32 devices in a mesh: group: 4 (over z), tp: 2 (over x), seq: 4 (over y, core).
Axes of the slice: x: 2, y: 2, z: 4, core: 2. Of those that a mesh axis runs over, the one named last changes fastest.
Arguments:
- queries: bfloat16 [8192, 8192], P(('group', 'seq'), 'tp'), may hold values from -8 to 8
- keys_values: bfloat16 [8192, 2048], P(('group', 'seq'), 'tp'), may hold values from -8 to 8
- prompt_lengths: int32 [3], replicated, may hold values from 1 to 2048, as said below
- block_lists: int32 [3, 16, 4], replicated, may hold values from -1 to 15, as said below
- page_owner: int32 [3, 16], replicated, may hold values from 0 to 3, as said below
- decode_prompts: int32 [512], replicated, may hold values from 0 to 2
- cache_lengths: int32 [512], replicated, may hold values from 1 to 2048, as said below
Outputs:
- attended: bfloat16 [8192, 8192], P(('group', 'seq'), 'tp')
- pages: bfloat16 [49152, 2048], P(('group', 'seq'), 'tp')
The draws below stay inside these ranges and needn't reach their ends.
Inputs may be any that keep to these rules, and one draw needn't show every extreme that they name: `prompt_lengths`: one prompt has exactly 2048 tokens. `block_lists`: entry 0 of a list is the query block itself; the other entries are distinct earlier blocks of the same prompt, then -1 where fewer than 3 earlier blocks exist. `page_owner`: among the 4 blocks b = s * 4 to s * 4 + 3 of one prompt, at most 2 share an owner, and for every prompt and s some owner (which may differ between prompts and s) takes exactly 2 of them. `cache_lengths`: at most the length of the sequence's prompt.
All inputs are finite; a program needn't handle non-finite values.
Results may differ from the reference program's by a relative error of at most 0.03.
Values may be sent and summed in bfloat16 or wider, within the bound.
A program may use at most 192 MiB of HBM per device.

```python
import math
import jax
import jax.numpy as jnp
from jax import lax

NH = 64
KVH = 8
HD = 128
SPAN = 2048
TILE = 128
TOPB = 4
STEPS = 4
NB = 16
PBLK = 4
MOSTB = 2
CAPS = 3072
DR = 128
DROWS = 512
TOTAL_ROWS = 8192
N_GROUP = 4
N_SEQ = 4


def prompt_setup(key):
    fullest_key = jax.random.fold_in(key, 201)
    length_key = jax.random.fold_in(key, 202)
    choice_key = jax.random.fold_in(key, 203)
    fullest = jax.random.randint(fullest_key, (), 0, N_GROUP - 1)
    lengths = jax.random.randint(length_key, (N_GROUP - 1,), 1, SPAN + 1)
    lengths = jnp.where(jnp.arange(N_GROUP - 1, dtype=jnp.int32) == fullest, SPAN, lengths).astype(jnp.int32)
    continued = jax.random.randint(choice_key, (DROWS,), 0, N_GROUP - 1)
    continued = continued.at[0].set(fullest).astype(jnp.int32)
    return (lengths, continued)


def draw_queries(key, part):
    key = jax.random.fold_in(key, 11)
    noise_key = jax.random.fold_in(key, 0)
    return jax.random.truncated_normal(noise_key, -8.0, 8.0, (TOTAL_ROWS, NH * HD), jnp.float32).astype(jnp.bfloat16)


def draw_keys_values(key, part):
    key = jax.random.fold_in(key, 13)
    return jax.random.truncated_normal(key, -8.0, 8.0, (TOTAL_ROWS, KVH * 2 * HD), jnp.float32).astype(jnp.bfloat16)


def draw_prompt_lengths(key, part):
    lengths, continued = prompt_setup(key)
    return lengths


def draw_decode_prompts(key, part):
    lengths, continued = prompt_setup(key)
    return continued


def draw_cache_lengths(key, part):
    lengths, continued = prompt_setup(key)
    key = jax.random.fold_in(key, 23)
    full_key, spread_key = jax.random.split(key, 2)
    limit = lengths[continued]
    whole = jax.random.randint(full_key, (DROWS,), 0, 4) == 0
    partial_length = 1 + jax.random.randint(spread_key, (DROWS,), 0, 1 << 20) % limit
    chosen = jnp.where(whole, limit, partial_length)
    return chosen.at[0].set(limit[0]).astype(jnp.int32)


def draw_block_lists(key, part):
    key = jax.random.fold_in(key, 17)
    raw = jax.random.randint(key, (N_GROUP - 1, NB, NB), 0, 1 << 20)
    candidate = jnp.arange(NB, dtype=jnp.int32)
    query_block = candidate.reshape(NB, 1)
    scored = jnp.where(candidate[None, :] < query_block, raw * NB + candidate[None, :], -1)
    ranked_scores, ranked_blocks = lax.top_k(scored, TOPB - 1)
    earlier = jnp.where(ranked_scores >= 0, ranked_blocks, -1).astype(jnp.int32)
    itself = jnp.broadcast_to(query_block[None], (N_GROUP - 1, NB, 1)).astype(jnp.int32)
    return jnp.concatenate([itself, earlier], axis=2)


def draw_page_owner(key, part):
    key = jax.random.fold_in(key, 19)
    busy_key, order_key, other_key = jax.random.split(key, 3)
    busiest = jax.random.randint(busy_key, (), 0, N_SEQ)
    raw = jax.random.randint(order_key, (N_GROUP - 1, N_SEQ, PBLK), 0, 1 << 20) * PBLK + jnp.arange(PBLK, dtype=jnp.int32)
    placing = jnp.argsort(jnp.argsort(raw, axis=2, stable=True), axis=2, stable=True)
    shifted = (busiest + 1 + jax.random.randint(other_key, (N_GROUP - 1, N_SEQ, PBLK), 0, N_SEQ - 1)) % N_SEQ
    owner = jnp.where(placing < MOSTB, busiest, shifted)
    return owner.reshape(N_GROUP - 1, NB).astype(jnp.int32)


def setup_inputs(seed: int = 0) -> dict:
    key_list = jax.random.split(jax.random.key(seed), 8)
    return {
        "queries": draw_queries(jax.random.fold_in(key_list[7], 71), 0),
        "keys_values": draw_keys_values(jax.random.fold_in(key_list[7], 71), 0),
        "prompt_lengths": draw_prompt_lengths(jax.random.fold_in(key_list[7], 71), 0),
        "block_lists": draw_block_lists(jax.random.fold_in(key_list[7], 71), 0),
        "page_owner": draw_page_owner(jax.random.fold_in(key_list[7], 71), 0),
        "decode_prompts": draw_decode_prompts(jax.random.fold_in(key_list[7], 71), 0),
        "cache_lengths": draw_cache_lengths(jax.random.fold_in(key_list[7], 71), 0),
    }


NEG = -1e+30

def page_table(prompt_lengths, page_owner, seq_count, tiles, capacity):
    prompts = page_owner.shape[0]
    owner_grid = page_owner.reshape(prompts, seq_count, tiles)
    block_ids = jnp.arange(seq_count * tiles, dtype=jnp.int32).reshape(1, seq_count, tiles)
    live_block = block_ids * TILE < prompt_lengths.reshape(prompts, 1, 1)
    local_ids = jnp.arange(tiles, dtype=jnp.int32)
    earlier = local_ids[None, :] < local_ids[:, None]
    same_owner = owner_grid[:, :, :, None] == owner_grid[:, :, None, :]
    order_rank = lax.optimization_barrier(jnp.sum((same_owner & live_block[:, :, None, :] & earlier[None, None]).astype(jnp.int32), axis=3))
    owner_ids = jnp.arange(seq_count, dtype=jnp.int32)
    slot_ids = jnp.arange(capacity, dtype=jnp.int32)
    matches = (owner_grid[..., None, None] == owner_ids[:, None]) & (order_rank[..., None, None] == slot_ids[None, :]) & live_block[..., None, None]
    return lax.optimization_barrier(jnp.sum(matches.astype(jnp.int32) * (block_ids[..., None, None] + 1), axis=2)) - 1

def attend(query, key_part, value_part, visible, score_scale):
    scores = jnp.einsum('mkgd,nkd->mkgn', query, key_part) * score_scale
    shown = visible[:, None, None, :]
    peak = lax.optimization_barrier(jnp.max(jnp.where(shown, scores, NEG), axis=3))
    raised = jnp.where(shown, jnp.exp(scores - peak[..., None]), 0.0)
    weight_sum = lax.optimization_barrier(jnp.sum(raised, axis=3))
    rounded = lax.optimization_barrier(raised.astype(jnp.bfloat16)).astype(query.dtype)
    mixed = jnp.einsum('mkgn,nkd->mkgd', rounded, value_part)
    return mixed / weight_sum[..., None]

def reference(queries, keys_values, prompt_lengths, block_lists, page_owner, decode_prompts, cache_lengths):
    prompts = N_GROUP - 1
    share = NH // KVH
    score_scale = 1.0 / math.sqrt(HD)
    query_all = queries.reshape(N_GROUP, SPAN, KVH, share, HD)
    pair_all = keys_values.reshape(N_GROUP, SPAN, KVH, 2, HD)

    def prefill_tile(index):
        prompt = (index // NB).astype(jnp.int32)
        block = (index % NB).astype(jnp.int32)
        zero_index = jnp.zeros((), jnp.int32)
        starts = (prompt, (block * TILE).astype(jnp.int32), zero_index, zero_index, zero_index)
        query = lax.dynamic_slice(query_all, starts, (1, TILE, KVH, share, HD))[0].astype(jnp.float32)
        chosen = lax.dynamic_index_in_dim(lax.dynamic_index_in_dim(block_lists, prompt, 0, False), block, 0, False)
        clamped = jnp.maximum(chosen, 0)
        tiles = lax.dynamic_index_in_dim(pair_all, prompt, 0, False).reshape(NB, TILE, KVH, 2, HD)
        picked = jnp.take(tiles, clamped, axis=0).reshape(TOPB * TILE, KVH, 2, HD).astype(jnp.float32)
        query_pos = block * TILE + jnp.arange(TILE, dtype=jnp.int32)
        key_pos = (clamped[:, None] * TILE + jnp.arange(TILE, dtype=jnp.int32)[None, :]).reshape(-1)
        listed = jnp.repeat(chosen >= 0, TILE)
        visible = listed[None, :] & (key_pos[None, :] <= query_pos[:, None])
        mixed = attend(query, picked[:, :, 0], picked[:, :, 1], visible, score_scale)
        length = lax.dynamic_index_in_dim(prompt_lengths, prompt, 0, False)
        mixed = jnp.where((query_pos < length)[:, None, None, None], mixed, 0.0)
        return mixed.reshape(TILE, NH * HD).astype(jnp.bfloat16)
    prefill_out = lax.map(prefill_tile, jnp.arange(prompts * NB, dtype=jnp.int32)).reshape(prompts * SPAN, NH * HD)
    decode_query = query_all[prompts].reshape(N_SEQ, STEPS, DR, KVH, share, HD)
    decode_query = jnp.transpose(decode_query, (0, 2, 1, 3, 4, 5)).reshape(DROWS, STEPS, KVH, share, HD)
    decode_pair = pair_all[prompts].reshape(N_SEQ, STEPS, DR, KVH, 2, HD)
    decode_pair = jnp.transpose(decode_pair, (0, 2, 1, 3, 4, 5)).reshape(DROWS, STEPS, KVH, 2, HD)
    step_ids = jnp.arange(STEPS, dtype=jnp.int32)
    own_visible = step_ids[None, :] <= step_ids[:, None]
    token_ids = jnp.arange(SPAN, dtype=jnp.int32)

    def decode_row(inputs):
        query, own_pair, prompt, limit = inputs
        cache = lax.dynamic_index_in_dim(pair_all, prompt, 0, False)
        key_part = jnp.concatenate([cache[:, :, 0], own_pair[:, :, 0]], axis=0).astype(jnp.float32)
        value_part = jnp.concatenate([cache[:, :, 1], own_pair[:, :, 1]], axis=0).astype(jnp.float32)
        cache_visible = jnp.broadcast_to((token_ids < limit)[None, :], (STEPS, SPAN))
        visible = jnp.concatenate([cache_visible, own_visible], axis=1)
        mixed = attend(query.astype(jnp.float32), key_part, value_part, visible, score_scale)
        return mixed.reshape(STEPS, NH * HD).astype(jnp.bfloat16)
    decode_out = lax.map(decode_row, (decode_query, decode_pair, decode_prompts, cache_lengths))
    decode_out = jnp.transpose(decode_out.reshape(N_SEQ, DR, STEPS, NH * HD), (0, 2, 1, 3)).reshape(SPAN, NH * HD)
    attended = jnp.concatenate([prefill_out, decode_out], axis=0)
    slot_block = jnp.transpose(page_table(prompt_lengths, page_owner, N_SEQ, PBLK, MOSTB), (2, 0, 1, 3))
    prompt_tiles = keys_values[:prompts * SPAN].reshape(prompts, NB, TILE, KVH * 2 * HD)
    prompt_index = jnp.broadcast_to(jnp.arange(prompts, dtype=jnp.int32)[None, :, None, None], slot_block.shape)
    gathered = prompt_tiles[prompt_index, jnp.maximum(slot_block, 0)]
    gathered = jnp.where(slot_block[..., None, None] >= 0, gathered, jnp.zeros_like(gathered))
    decode_pages = gathered.reshape(N_SEQ * CAPS, KVH * 2 * HD)
    empty_pages = jnp.zeros((prompts * N_SEQ * CAPS, KVH * 2 * HD), jnp.bfloat16)
    pages = jnp.concatenate([empty_pages, decode_pages], axis=0)
    return (attended, pages)
```

```python
import functools
import math

import jax
import jax.numpy as jnp
from jax import lax
from jax.experimental import pallas as pl
from jax.experimental.pallas import tpu as pltpu
from jax.sharding import PartitionSpec as P

KVH = 8
HD = 128
TILE = 128
STEPS = 4
PACK = 16
KEYS = 512


NEG = -1e30
VMEM = 44 * 2**20


def swapped(value, axis, apart):
    mask = 2**apart
    pairs = [(source, source ^ mask) for source in range(lax.axis_size(axis))]
    return lax.ppermute(value, axis, pairs)


def page_table(prompt_lengths, page_owner, seq_count, tiles, capacity):
    prompts = page_owner.shape[0]
    owner_grid = page_owner.reshape(prompts, seq_count, tiles)
    block_ids = jnp.arange(seq_count * tiles, dtype=jnp.int32).reshape(1, seq_count, tiles)
    live_block = block_ids * TILE < prompt_lengths.reshape(prompts, 1, 1)
    local_ids = jnp.arange(tiles, dtype=jnp.int32)
    earlier = local_ids[None, :] < local_ids[:, None]
    same_owner = owner_grid[:, :, :, None] == owner_grid[:, :, None, :]
    order_rank = jnp.sum(
        (same_owner & live_block[:, :, None, :] & earlier[None, None]).astype(jnp.int32), axis=3
    )
    owner_ids = jnp.arange(seq_count, dtype=jnp.int32)
    slot_ids = jnp.arange(capacity, dtype=jnp.int32)
    matches = (
        (owner_grid[..., None, None] == owner_ids[:, None])
        & (order_rank[..., None, None] == slot_ids[None, :])
        & live_block[..., None, None]
    )
    return jnp.sum(matches.astype(jnp.int32) * (block_ids[..., None, None] + 1), axis=2) - 1


def prefill_kernel(lists_ref, info_ref, q_ref, kv_ref, out_ref, *, share, topb, scale):
    tile = pl.program_id(1)
    number = info_ref[0] + tile
    length = info_ref[1]
    alive = number * TILE < length

    @pl.when(alive)
    def _():
        q = jnp.concatenate([q_ref[:, h * HD : (h + 1) * HD] for h in range(share)], axis=0)
        starts = [
            pl.multiple_of(jnp.maximum(lists_ref[tile * topb + c], 0) * TILE, TILE)
            for c in range(topb)
        ]
        k = jnp.concatenate([kv_ref[pl.ds(s, TILE), :HD] for s in starts], axis=0)
        v = jnp.concatenate([kv_ref[pl.ds(s, TILE), HD:] for s in starts], axis=0)
        scores = (
            lax.dot_general(q, k, (((1,), (1,)), ((), ())), preferred_element_type=jnp.float32)
            * scale
        )
        key_at = lax.broadcasted_iota(jnp.int32, (1, TILE), 1)
        positions = jnp.concatenate(
            [
                jnp.where(lists_ref[tile * topb + c] >= 0, starts[c] + key_at, 2**30)
                for c in range(topb)
            ],
            axis=1,
        )
        at = lax.broadcasted_iota(jnp.int32, (TILE, 1), 0) + number * TILE
        query_at = jnp.concatenate([at] * share, axis=0)
        scores = jnp.where(positions <= query_at, scores, NEG)
        peak = jnp.max(scores, axis=1, keepdims=True)
        raised = jnp.exp(scores - peak)
        total = jnp.sum(raised, axis=1, keepdims=True)
        mixed = jnp.dot(raised.astype(jnp.bfloat16), v, preferred_element_type=jnp.float32)
        mixed = jnp.where(query_at < length, mixed / total, 0.0).astype(jnp.bfloat16)
        for h in range(share):
            out_ref[:, h * HD : (h + 1) * HD] = mixed[h * TILE : (h + 1) * TILE]

    @pl.when(jnp.logical_not(alive))
    def _():
        out_ref[...] = jnp.zeros_like(out_ref)


def prefill(lists, info, queries, kv_whole, kv_heads, share, scale):
    rows = queries.shape[0]
    topb = lists.shape[1]
    width = share * HD
    cost = rows * kv_heads * share * topb * TILE
    return pl.pallas_call(
        functools.partial(prefill_kernel, share=share, topb=topb, scale=scale),
        grid_spec=pltpu.PrefetchScalarGridSpec(
            num_scalar_prefetch=2,
            grid=(kv_heads, rows // TILE),
            in_specs=[
                pl.BlockSpec((TILE, width), lambda e, t, *_: (t, e)),
                pl.BlockSpec((kv_whole.shape[0], 2 * HD), lambda e, t, *_: (0, e)),
            ],
            out_specs=pl.BlockSpec((TILE, width), lambda e, t, *_: (t, e)),
        ),
        out_shape=jax.ShapeDtypeStruct(queries.shape, jnp.bfloat16),
        compiler_params=pltpu.CompilerParams(vmem_limit_bytes=VMEM),
        cost_estimate=pl.CostEstimate(
            flops=4 * HD * cost, bytes_accessed=4 * queries.size, transcendentals=cost
        ),
        name="prefill",
    )(lists.reshape(-1), info, queries, kv_whole)


def decode_kernel(
    meta_ref, slots_ref, *refs, first, last, prompt, prompts, slots, share, scale, tile_count
):
    refs = list(refs)
    q_ref, own_ref, len_ref, kv_ref = refs[:4]
    refs = refs[4:]
    if not first:
        prev_ref = refs.pop(0)
        refs.pop(0)
    if last:
        back_ref = refs.pop(0)
        done_ref = refs.pop(0)
    out_ref, pages_ref, peak_ref, acc_ref = refs[:4]
    buf = refs[4] if last else out_ref

    for k in range(slots):
        block = slots_ref[prompt * slots + k]
        rows = pl.ds(k * TILE, TILE)

        @pl.when(block >= 0)
        def _():
            at = pl.multiple_of(block * TILE, TILE)
            pages_ref[rows, :] = kv_ref[pl.ds(at, TILE), :]

        @pl.when(block < 0)
        def _():
            pages_ref[rows, :] = jnp.zeros((TILE, 2 * HD), jnp.bfloat16)

    is_decode = meta_ref[prompts + 1] > 0

    @pl.when(is_decode)
    def _():
        if first:
            buf[...] = jnp.zeros_like(buf)
        else:
            buf[...] = prev_ref[...]

    copies = STEPS * share
    height = copies * PACK
    row_at = lax.broadcasted_iota(jnp.int32, (height, 1), 0)

    def tile_step(t, carry):
        base = pl.multiple_of(t * PACK, PACK)
        rows = pl.ds(base, PACK)
        q = jnp.concatenate(
            [q_ref[j, rows, h * HD : (h + 1) * HD] for j in range(STEPS) for h in range(share)],
            axis=0,
        )
        wide = q.astype(jnp.float32)
        own = []
        for i in range(STEPS):
            key = own_ref[i, rows, :HD].astype(jnp.float32)
            key = jnp.concatenate([key] * copies, axis=0)
            score = jnp.sum(wide * key, axis=1, keepdims=True) * scale
            own.append(jnp.where(row_at >= i * share * PACK, score, NEG))
        peak = functools.reduce(jnp.maximum, own)
        total = jnp.zeros_like(peak)
        mixed = jnp.zeros((height, HD), jnp.float32)
        for i in range(STEPS):
            weight = jnp.exp(own[i] - peak)
            value = own_ref[i, rows, HD:].astype(jnp.float32)
            value = jnp.concatenate([value] * copies, axis=0)
            total = total + weight
            mixed = mixed + weight.astype(jnp.bfloat16).astype(jnp.float32) * value
        peak_ref[...] = jnp.broadcast_to(peak, (height, HD))
        acc_ref[:, :HD] = mixed
        acc_ref[:, HD:] = jnp.broadcast_to(total, (height, HD))
        limit = jnp.concatenate([len_ref[rows, :]] * copies, axis=0)
        longest = meta_ref[prompts + 2 + t]

        def key_step(b, carry):
            at = pl.multiple_of(b * KEYS, KEYS)
            k = kv_ref[pl.ds(at, KEYS), :HD]
            v = kv_ref[pl.ds(at, KEYS), HD:]
            v = jnp.concatenate([v, jnp.ones_like(v)], axis=1)
            scores = (
                lax.dot_general(q, k, (((1,), (1,)), ((), ())), preferred_element_type=jnp.float32)
                * scale
            )
            position = lax.broadcasted_iota(jnp.int32, (1, KEYS), 1) + at
            scores = jnp.where(position < limit, scores, NEG)
            before = peak_ref[:, :1]
            after = jnp.maximum(before, jnp.max(scores, axis=1, keepdims=True))
            weights = jnp.exp(scores - after).astype(jnp.bfloat16)
            decay = jnp.exp(before - after)
            peak_ref[...] = jnp.broadcast_to(after, (height, HD))
            acc_ref[...] = acc_ref[...] * decay + jnp.dot(
                weights, v, preferred_element_type=jnp.float32
            )
            return carry

        lax.fori_loop(0, lax.div(longest + KEYS - 1, KEYS), key_step, 0)
        out = (acc_ref[:, :HD] / acc_ref[:, HD:]).astype(jnp.bfloat16)
        for j in range(STEPS):
            for h in range(share):
                n = (j * share + h) * PACK
                buf[j, rows, h * HD : (h + 1) * HD] = out[n : n + PACK]
        return carry

    lax.fori_loop(meta_ref[prompt], meta_ref[prompt + 1], tile_step, 0)

    if last:

        @pl.when(is_decode)
        def _():
            count = out_ref.shape[0] // STEPS
            for j in range(STEPS):
                out_ref[j * count : (j + 1) * count, :] = jnp.dot(
                    back_ref[...], buf[j], preferred_element_type=jnp.float32
                ).astype(jnp.bfloat16)

        @pl.when(jnp.logical_not(is_decode))
        def _():
            out_ref[...] = done_ref[...]


def decode(
    meta,
    slot_blocks,
    q_sorted,
    own_sorted,
    lens,
    kv,
    prev,
    pages,
    back,
    done,
    prompt,
    prompts,
    kv_heads,
    share,
    scale,
):
    first, last = prev is None, back is not None
    places = q_sorted.shape[1]
    slots = slot_blocks.shape[1]
    width = share * HD
    cols = kv_heads * 2 * HD
    in_specs = [
        pl.BlockSpec((STEPS, places, width), lambda e, *_: (0, 0, e)),
        pl.BlockSpec((STEPS, places, 2 * HD), lambda e, *_: (0, 0, e)),
        pl.BlockSpec((places, 1), lambda e, *_: (0, 0)),
        pl.BlockSpec((kv.shape[0], 2 * HD), lambda e, *_: (0, e)),
    ]
    args = [q_sorted, own_sorted, lens, kv]
    aliases = {}
    if not first:
        in_specs += [
            pl.BlockSpec((STEPS, places, width), lambda e, *_: (0, 0, e)),
            pl.BlockSpec(memory_space=pl.ANY),
        ]
        aliases[2 + len(args) + 1] = 1
        args += [prev, pages]
    height = STEPS * share * PACK
    scratch = [pltpu.VMEM((height, HD), jnp.float32), pltpu.VMEM((height, 2 * HD), jnp.float32)]
    out_spec = pl.BlockSpec((STEPS, places, width), lambda e, *_: (0, 0, e))
    out_shape = jax.ShapeDtypeStruct(q_sorted.shape, jnp.bfloat16)
    if last:
        in_specs += [
            pl.BlockSpec(back.shape, lambda e, *_: (0, 0)),
            pl.BlockSpec((done.shape[0], width), lambda e, *_: (0, e)),
        ]
        args += [back, done]
        out_spec = pl.BlockSpec((done.shape[0], width), lambda e, *_: (0, e))
        out_shape = jax.ShapeDtypeStruct(done.shape, jnp.bfloat16)
        scratch.append(pltpu.VMEM((STEPS, places, width), jnp.bfloat16))
    cost = STEPS * places * kv_heads * share * kv.shape[0] // prompts
    return pl.pallas_call(
        functools.partial(
            decode_kernel,
            first=first,
            last=last,
            prompt=prompt,
            prompts=prompts,
            slots=slots,
            share=share,
            scale=scale,
            tile_count=places // PACK,
        ),
        grid_spec=pltpu.PrefetchScalarGridSpec(
            num_scalar_prefetch=2,
            grid=(kv_heads,),
            in_specs=in_specs,
            out_specs=[
                out_spec,
                pl.BlockSpec((slots * TILE, 2 * HD), lambda e, *_: (prompt, e)),
            ],
            scratch_shapes=scratch,
        ),
        out_shape=[
            out_shape,
            jax.ShapeDtypeStruct((prompts * slots * TILE, cols), jnp.bfloat16),
        ],
        input_output_aliases=aliases,
        compiler_params=pltpu.CompilerParams(vmem_limit_bytes=VMEM),
        cost_estimate=pl.CostEstimate(
            flops=4 * HD * cost,
            bytes_accessed=2 * (3 * q_sorted.size + 2 * kv.size),
            transcendentals=cost,
        ),
        name=f"decode_{prompt}",
    )(meta, slot_blocks.reshape(-1), *args)


def body(
    queries, keys_values, prompt_lengths, block_lists, page_owner, decode_prompts, cache_lengths
):
    tp_size = lax.axis_size("tp")
    seq_size = lax.axis_size("seq")
    group_size = lax.axis_size("group")
    group_id = lax.axis_index("group")
    seq_id = lax.axis_index("seq")
    tp_id = lax.axis_index("tp")
    rows_dev = queries.shape[0]
    heads_dev = queries.shape[1] // HD
    kv_heads = max(KVH // tp_size, 1)
    share = heads_dev // kv_heads
    prompts = group_size - 1
    is_decode = group_id == prompts
    tiles = rows_dev // TILE
    capacity = max(2, tiles // 2)
    score_scale = 1.0 / math.sqrt(HD)
    prompt_index = jnp.minimum(group_id, prompts - 1)
    if tp_size == 2 * KVH:
        partner = swapped(keys_values, "tp", 0)
        holds_keys = tp_id % 2 == 0
        key_part = jnp.where(holds_keys, keys_values, partner)
        value_part = jnp.where(holds_keys, partner, keys_values)
        kv_flat = jnp.concatenate([key_part, value_part], axis=1)
    else:
        kv_flat = keys_values

    onward = [(g, g + 1) for g in range(group_size - 1)]
    hops = [kv_flat]
    for _ in range(prompts):
        hops.append(lax.ppermute(hops[-1], "group", onward))
    wholes = [lax.all_gather(piece, "seq", axis=0, tiled=True) for piece in hops]

    length = lax.dynamic_index_in_dim(prompt_lengths, prompt_index, 0, False)
    length = jnp.where(is_decode, 0, length)
    lists = lax.dynamic_index_in_dim(block_lists, prompt_index, 0, False)
    my_lists = lax.dynamic_slice_in_dim(lists, seq_id * tiles, tiles, 0)
    info = jnp.stack([seq_id * tiles, length]).astype(jnp.int32)

    count = rows_dev // STEPS
    tile_count = (count + (PACK - 1) * prompts) // PACK
    places = tile_count * PACK
    own_prompt = lax.dynamic_slice_in_dim(decode_prompts, seq_id * count, count)
    own_len = lax.dynamic_slice_in_dim(cache_lengths, seq_id * count, count)
    ids = jnp.arange(count, dtype=jnp.int32)
    ahead = (own_prompt[None, :] == own_prompt[:, None]) & (
        (own_len[None, :] < own_len[:, None])
        | ((own_len[None, :] == own_len[:, None]) & (ids[None, :] < ids[:, None]))
    )
    rank = jnp.sum(ahead.astype(jnp.int32), axis=1)
    prompt_ids = jnp.arange(prompts, dtype=jnp.int32)
    members = jnp.sum((own_prompt[None, :] == prompt_ids[:, None]).astype(jnp.int32), axis=1)
    used = (members + PACK - 1) // PACK
    before = prompt_ids[None, :] < jnp.arange(prompts + 1, dtype=jnp.int32)[:, None]
    starts = jnp.sum(jnp.where(before, used[None, :], 0), axis=1)
    place = rank + PACK * jnp.sum(
        jnp.where(own_prompt[:, None] == prompt_ids[None, :], starts[None, :prompts], 0), axis=1
    )
    chosen = jnp.arange(places, dtype=jnp.int32)[:, None] == place[None, :]
    perm = chosen.astype(jnp.bfloat16)
    lens = jnp.sum(jnp.where(chosen, own_len[None, :], 0), axis=1)
    longest = jnp.max(lens.reshape(tile_count, PACK), axis=1)
    starts = jnp.where(is_decode, starts, 0)
    meta = jnp.concatenate(
        [starts, is_decode.astype(jnp.int32)[None], longest]
    ).astype(jnp.int32)
    q_sorted = jnp.einsum(
        "sr,jrc->jsc",
        perm,
        queries.reshape(STEPS, count, -1),
        preferred_element_type=jnp.float32,
    ).astype(jnp.bfloat16)
    own_sorted = jnp.einsum(
        "sr,jrc->jsc",
        perm,
        kv_flat.reshape(STEPS, count, -1),
        preferred_element_type=jnp.float32,
    ).astype(jnp.bfloat16)

    slot_table = page_table(prompt_lengths, page_owner, seq_size, tiles, capacity)
    mine = lax.dynamic_index_in_dim(slot_table, seq_id, 2, False)
    mine = jnp.where(is_decode, mine, -1).reshape(prompts, -1)

    done = prefill(my_lists, info, queries, wholes[0], kv_heads, share, score_scale)
    out = pages = None
    for hop in range(1, prompts + 1):
        final = hop == prompts
        out, pages = decode(
            meta,
            mine,
            q_sorted,
            own_sorted,
            lens[:, None],
            wholes[hop],
            out,
            pages,
            perm.T if final else None,
            done if final else None,
            prompts - hop,
            prompts,
            kv_heads,
            share,
            score_scale,
        )
    if tp_size == 2 * KVH:
        pages = lax.dynamic_slice_in_dim(pages, tp_id % 2 * HD, HD, 1)
    return (out, pages)


def solution(mesh):
    placed = (P(("group", "seq"), "tp"), P(("group", "seq"), "tp"), P(), P(), P(), P(), P())
    return jax.shard_map(
        body,
        mesh=mesh,
        in_specs=placed,
        out_specs=(P(("group", "seq"), "tp"), P(("group", "seq"), "tp")),
        check_vma=False,
    )
```

```python
import functools
import math

import jax
import jax.numpy as jnp
from jax import lax
from jax.experimental import pallas as pl
from jax.experimental.pallas import tpu as pltpu
from jax.sharding import PartitionSpec as P

KVH = 8
HD = 128
TILE = 128
STEPS = 4
PACK = 16
KEYS = 512
HALVES = 4


NEG = -1e30
VMEM = 44 * 2**20


def swapped(value, axis, apart):
    mask = 2**apart
    pairs = [(source, source ^ mask) for source in range(lax.axis_size(axis))]
    return lax.ppermute(value, axis, pairs)


def page_table(prompt_lengths, page_owner, seq_count, tiles, capacity):
    prompts = page_owner.shape[0]
    owner_grid = page_owner.reshape(prompts, seq_count, tiles)
    block_ids = jnp.arange(seq_count * tiles, dtype=jnp.int32).reshape(1, seq_count, tiles)
    live_block = block_ids * TILE < prompt_lengths.reshape(prompts, 1, 1)
    local_ids = jnp.arange(tiles, dtype=jnp.int32)
    earlier = local_ids[None, :] < local_ids[:, None]
    same_owner = owner_grid[:, :, :, None] == owner_grid[:, :, None, :]
    order_rank = jnp.sum(
        (same_owner & live_block[:, :, None, :] & earlier[None, None]).astype(jnp.int32), axis=3
    )
    owner_ids = jnp.arange(seq_count, dtype=jnp.int32)
    slot_ids = jnp.arange(capacity, dtype=jnp.int32)
    matches = (
        (owner_grid[..., None, None] == owner_ids[:, None])
        & (order_rank[..., None, None] == slot_ids[None, :])
        & live_block[..., None, None]
    )
    return jnp.sum(matches.astype(jnp.int32) * (block_ids[..., None, None] + 1), axis=2) - 1


def lay_out(pieces, seq_id, kv_ref):
    rows = pieces[0].shape[0]
    for x, piece in enumerate(pieces):
        at = pl.multiple_of((seq_id ^ x) * rows, TILE)
        kv_ref[pl.ds(at, rows), :] = piece[...]


def prefill_kernel(lists_ref, info_ref, q_ref, *refs, share, topb, scale):
    *pieces, out_ref, kv_ref = refs
    tile = pl.program_id(1)

    @pl.when(tile == 0)
    def _():
        lay_out(pieces, info_ref[2], kv_ref)

    number = info_ref[0] + tile
    length = info_ref[1]
    alive = number * TILE < length

    @pl.when(alive)
    def _():
        q = jnp.concatenate([q_ref[:, h * HD : (h + 1) * HD] for h in range(share)], axis=0)
        starts = [
            pl.multiple_of(jnp.maximum(lists_ref[tile * topb + c], 0) * TILE, TILE)
            for c in range(topb)
        ]
        k = jnp.concatenate([kv_ref[pl.ds(s, TILE), :HD] for s in starts], axis=0)
        v = jnp.concatenate([kv_ref[pl.ds(s, TILE), HD:] for s in starts], axis=0)
        scores = (
            lax.dot_general(q, k, (((1,), (1,)), ((), ())), preferred_element_type=jnp.float32)
            * scale
        )
        key_at = lax.broadcasted_iota(jnp.int32, (1, TILE), 1)
        positions = jnp.concatenate(
            [
                jnp.where(lists_ref[tile * topb + c] >= 0, starts[c] + key_at, 2**30)
                for c in range(topb)
            ],
            axis=1,
        )
        at = lax.broadcasted_iota(jnp.int32, (TILE, 1), 0) + number * TILE
        query_at = jnp.concatenate([at] * share, axis=0)
        scores = jnp.where(positions <= query_at, scores, NEG)
        peak = jnp.max(scores, axis=1, keepdims=True)
        raised = jnp.exp(scores - peak)
        total = jnp.sum(raised, axis=1, keepdims=True)
        mixed = jnp.dot(raised.astype(jnp.bfloat16), v, preferred_element_type=jnp.float32)
        mixed = jnp.where(query_at < length, mixed / total, 0.0).astype(jnp.bfloat16)
        for h in range(share):
            out_ref[:, h * HD : (h + 1) * HD] = mixed[h * TILE : (h + 1) * TILE]

    @pl.when(jnp.logical_not(alive))
    def _():
        out_ref[...] = jnp.zeros_like(out_ref)


def prefill(lists, info, queries, pieces, kv_heads, share, scale):
    rows = queries.shape[0]
    topb = lists.shape[1]
    width = share * HD
    cost = rows * kv_heads * share * topb * TILE
    return pl.pallas_call(
        functools.partial(prefill_kernel, share=share, topb=topb, scale=scale),
        grid_spec=pltpu.PrefetchScalarGridSpec(
            num_scalar_prefetch=2,
            grid=(kv_heads, rows // TILE),
            in_specs=[
                pl.BlockSpec((TILE, width), lambda e, t, *_: (t, e)),
                *[pl.BlockSpec((rows, 2 * HD), lambda e, t, *_: (0, e)) for _ in pieces],
            ],
            out_specs=pl.BlockSpec((TILE, width), lambda e, t, *_: (t, e)),
            scratch_shapes=[pltpu.VMEM((rows * len(pieces), 2 * HD), jnp.bfloat16)],
        ),
        out_shape=jax.ShapeDtypeStruct(queries.shape, jnp.bfloat16),
        compiler_params=pltpu.CompilerParams(vmem_limit_bytes=VMEM),
        cost_estimate=pl.CostEstimate(
            flops=4 * HD * cost, bytes_accessed=4 * queries.size, transcendentals=cost
        ),
        name="prefill",
    )(lists.reshape(-1), info, queries, *pieces)


def decode_kernel(
    meta_ref, slots_ref, *refs, first, last, prompt, prompts, slots, share, scale, parts
):
    refs = list(refs)
    q_ref, own_ref, len_ref = refs[:3]
    pieces = refs[3 : 3 + parts]
    refs = refs[3 + parts :]
    if not first:
        prev_ref = refs.pop(0)
        refs.pop(0)
    if last:
        back_ref = refs.pop(0)
        done_ref = refs.pop(0)
    out_ref, pages_ref, peak_ref, acc_ref, limit_ref, kv_ref = refs[:6]
    buf = refs[6] if last else out_ref
    lay_out(pieces, meta_ref[prompts + 2 + len_ref.shape[0] // PACK], kv_ref)

    for k in range(slots):
        block = slots_ref[prompt * slots + k]
        rows = pl.ds(k * TILE, TILE)

        @pl.when(block >= 0)
        def _():
            at = pl.multiple_of(block * TILE, TILE)
            pages_ref[rows, :] = kv_ref[pl.ds(at, TILE), :]

        @pl.when(block < 0)
        def _():
            pages_ref[rows, :] = jnp.zeros((TILE, 2 * HD), jnp.bfloat16)

    is_decode = meta_ref[prompts + 1] > 0

    @pl.when(is_decode)
    def _():
        if first:
            buf[...] = jnp.zeros_like(buf)
        else:
            buf[...] = prev_ref[...]

    scale = scale * math.log2(math.e)
    copies = STEPS * share
    height = copies * PACK
    row_at = lax.broadcasted_iota(jnp.int32, (height, 1), 0)

    def tile_step(t, carry):
        base = pl.multiple_of(t * PACK, PACK)
        rows = pl.ds(base, PACK)
        q = jnp.concatenate(
            [q_ref[j, rows, h * HD : (h + 1) * HD] for j in range(STEPS) for h in range(share)],
            axis=0,
        )
        wide = q.astype(jnp.float32)
        own = []
        for i in range(STEPS):
            key = own_ref[i, rows, :HD].astype(jnp.float32)
            key = jnp.concatenate([key] * copies, axis=0)
            score = jnp.sum(wide * key, axis=1, keepdims=True) * scale
            own.append(jnp.where(row_at >= i * share * PACK, score, NEG))
        peak = functools.reduce(jnp.maximum, own)
        total = jnp.zeros_like(peak)
        mixed = jnp.zeros((height, HD), jnp.float32)
        for i in range(STEPS):
            weight = jnp.exp2(own[i] - peak)
            value = own_ref[i, rows, HD:].astype(jnp.float32)
            value = jnp.concatenate([value] * copies, axis=0)
            total = total + weight
            mixed = mixed + weight.astype(jnp.bfloat16).astype(jnp.float32) * value
        peak_ref[...] = jnp.broadcast_to(peak, (height, HD))
        acc_ref[:, :HD] = mixed
        acc_ref[:, HD:] = jnp.broadcast_to(total, (height, HD))
        limit = jnp.broadcast_to(len_ref[rows, :], (PACK, HD))
        limit_ref[...] = jnp.concatenate([limit] * copies, axis=0)
        longest = meta_ref[prompts + 2 + t]
        half = height // HALVES

        def key_step(b, carry):
            at = pl.multiple_of(b * KEYS, KEYS)
            k = kv_ref[pl.ds(at, KEYS), :HD]
            v = kv_ref[pl.ds(at, KEYS), HD:]
            v = jnp.concatenate([v, jnp.ones_like(v)], axis=1)
            lane = lax.broadcasted_iota(jnp.int32, (half, HD), 1)
            for n in range(HALVES):
                part = slice(n * half, (n + 1) * half)
                scores = lax.dot_general(
                    q[part], k, (((1,), (1,)), ((), ())), preferred_element_type=jnp.float32
                )
                limit = limit_ref[part, :] - at
                chunks = [
                    jnp.where(
                        lane + c * HD < limit, scores[:, c * HD : (c + 1) * HD] * scale, NEG
                    )
                    for c in range(KEYS // HD)
                ]
                before = peak_ref[part, :]
                top = jnp.max(functools.reduce(jnp.maximum, chunks), axis=1, keepdims=True)
                after = jnp.maximum(before, jnp.broadcast_to(top, (half, HD)))
                weights = jnp.concatenate(
                    [jnp.exp2(chunk - after).astype(jnp.bfloat16) for chunk in chunks], axis=1
                )
                decay = jnp.exp2(before - after)
                peak_ref[part, :] = after
                added = jnp.dot(weights, v, preferred_element_type=jnp.float32)
                acc_ref[part, :HD] = acc_ref[part, :HD] * decay + added[:, :HD]
                acc_ref[part, HD:] = acc_ref[part, HD:] * decay + added[:, HD:]
            return carry

        lax.fori_loop(0, lax.div(longest + KEYS - 1, KEYS), key_step, 0)
        out = (acc_ref[:, :HD] / acc_ref[:, HD:]).astype(jnp.bfloat16)
        for j in range(STEPS):
            for h in range(share):
                n = (j * share + h) * PACK
                buf[j, rows, h * HD : (h + 1) * HD] = out[n : n + PACK]
        return carry

    lax.fori_loop(meta_ref[prompt], meta_ref[prompt + 1], tile_step, 0)

    if last:

        @pl.when(is_decode)
        def _():
            count = out_ref.shape[0] // STEPS
            for j in range(STEPS):
                out_ref[j * count : (j + 1) * count, :] = jnp.dot(
                    back_ref[...], buf[j], preferred_element_type=jnp.float32
                ).astype(jnp.bfloat16)

        @pl.when(jnp.logical_not(is_decode))
        def _():
            out_ref[...] = done_ref[...]


def decode(
    meta,
    slot_blocks,
    q_sorted,
    own_sorted,
    lens,
    pieces,
    prev,
    pages,
    back,
    done,
    prompt,
    prompts,
    kv_heads,
    share,
    scale,
):
    first, last = prev is None, back is not None
    places = q_sorted.shape[1]
    slots = slot_blocks.shape[1]
    width = share * HD
    cols = kv_heads * 2 * HD
    in_specs = [
        pl.BlockSpec((STEPS, places, width), lambda e, *_: (0, 0, e)),
        pl.BlockSpec((STEPS, places, 2 * HD), lambda e, *_: (0, 0, e)),
        pl.BlockSpec((places, 1), lambda e, *_: (0, 0)),
        *[pl.BlockSpec((piece.shape[0], 2 * HD), lambda e, *_: (0, e)) for piece in pieces],
    ]
    args = [q_sorted, own_sorted, lens, *pieces]
    span = sum(piece.shape[0] for piece in pieces)
    aliases = {}
    if not first:
        in_specs += [
            pl.BlockSpec((STEPS, places, width), lambda e, *_: (0, 0, e)),
            pl.BlockSpec(memory_space=pl.ANY),
        ]
        aliases[2 + len(args) + 1] = 1
        args += [prev, pages]
    height = STEPS * share * PACK
    scratch = [
        pltpu.VMEM((height, HD), jnp.float32),
        pltpu.VMEM((height, 2 * HD), jnp.float32),
        pltpu.VMEM((height, HD), jnp.int32),
        pltpu.VMEM((span, 2 * HD), jnp.bfloat16),
    ]
    out_spec = pl.BlockSpec((STEPS, places, width), lambda e, *_: (0, 0, e))
    out_shape = jax.ShapeDtypeStruct(q_sorted.shape, jnp.bfloat16)
    if last:
        in_specs += [
            pl.BlockSpec(back.shape, lambda e, *_: (0, 0)),
            pl.BlockSpec((done.shape[0], width), lambda e, *_: (0, e)),
        ]
        args += [back, done]
        out_spec = pl.BlockSpec((done.shape[0], width), lambda e, *_: (0, e))
        out_shape = jax.ShapeDtypeStruct(done.shape, jnp.bfloat16)
        scratch.append(pltpu.VMEM((STEPS, places, width), jnp.bfloat16))
    cost = STEPS * places * kv_heads * share * span
    return pl.pallas_call(
        functools.partial(
            decode_kernel,
            first=first,
            last=last,
            prompt=prompt,
            prompts=prompts,
            slots=slots,
            share=share,
            scale=scale,
            parts=len(pieces),
        ),
        grid_spec=pltpu.PrefetchScalarGridSpec(
            num_scalar_prefetch=2,
            grid=(kv_heads,),
            in_specs=in_specs,
            out_specs=[
                out_spec,
                pl.BlockSpec((slots * TILE, 2 * HD), lambda e, *_: (prompt, e)),
            ],
            scratch_shapes=scratch,
        ),
        out_shape=[
            out_shape,
            jax.ShapeDtypeStruct((prompts * slots * TILE, cols), jnp.bfloat16),
        ],
        input_output_aliases=aliases,
        compiler_params=pltpu.CompilerParams(vmem_limit_bytes=VMEM),
        cost_estimate=pl.CostEstimate(
            flops=4 * HD * cost,
            bytes_accessed=2 * (3 * q_sorted.size + 2 * span * cols),
            transcendentals=cost,
        ),
        name=f"decode_{prompt}",
    )(meta, slot_blocks.reshape(-1), *args)


def body(
    queries, keys_values, prompt_lengths, block_lists, page_owner, decode_prompts, cache_lengths
):
    tp_size = lax.axis_size("tp")
    seq_size = lax.axis_size("seq")
    group_size = lax.axis_size("group")
    group_id = lax.axis_index("group")
    seq_id = lax.axis_index("seq")
    tp_id = lax.axis_index("tp")
    rows_dev = queries.shape[0]
    heads_dev = queries.shape[1] // HD
    kv_heads = max(KVH // tp_size, 1)
    share = heads_dev // kv_heads
    prompts = group_size - 1
    is_decode = group_id == prompts
    tiles = rows_dev // TILE
    capacity = max(2, tiles // 2)
    score_scale = 1.0 / math.sqrt(HD)
    prompt_index = jnp.minimum(group_id, prompts - 1)
    if tp_size == 2 * KVH:
        partner = swapped(keys_values, "tp", 0)
        holds_keys = tp_id % 2 == 0
        key_part = jnp.where(holds_keys, keys_values, partner)
        value_part = jnp.where(holds_keys, partner, keys_values)
        kv_flat = jnp.concatenate([key_part, value_part], axis=1)
    else:
        kv_flat = keys_values

    onward = [(g, g + 1) for g in range(group_size - 1)]
    hops = [kv_flat]
    for _ in range(prompts):
        hops.append(lax.ppermute(hops[-1], "group", onward))
    wholes = []
    for hop in range(1, prompts + 1):
        piece = jnp.where(is_decode, hops[hop], kv_flat) if hop == 1 else hops[hop]
        pieces = [piece]
        apart = 0
        while len(pieces) < seq_size:
            pieces += [swapped(held, "seq", apart) for held in pieces]
            apart += 1
        wholes.append(pieces)

    length = lax.dynamic_index_in_dim(prompt_lengths, prompt_index, 0, False)
    length = jnp.where(is_decode, 0, length)
    lists = lax.dynamic_index_in_dim(block_lists, prompt_index, 0, False)
    my_lists = lax.dynamic_slice_in_dim(lists, seq_id * tiles, tiles, 0)
    info = jnp.stack([seq_id * tiles, length, seq_id]).astype(jnp.int32)

    count = rows_dev // STEPS
    tile_count = (count + (PACK - 1) * prompts) // PACK
    places = tile_count * PACK
    own_prompt = lax.dynamic_slice_in_dim(decode_prompts, seq_id * count, count)
    own_len = lax.dynamic_slice_in_dim(cache_lengths, seq_id * count, count)
    ids = jnp.arange(count, dtype=jnp.int32)
    ahead = (own_prompt[None, :] == own_prompt[:, None]) & (
        (own_len[None, :] < own_len[:, None])
        | ((own_len[None, :] == own_len[:, None]) & (ids[None, :] < ids[:, None]))
    )
    rank = jnp.sum(ahead.astype(jnp.int32), axis=1)
    prompt_ids = jnp.arange(prompts, dtype=jnp.int32)
    members = jnp.sum((own_prompt[None, :] == prompt_ids[:, None]).astype(jnp.int32), axis=1)
    used = (members + PACK - 1) // PACK
    before = prompt_ids[None, :] < jnp.arange(prompts + 1, dtype=jnp.int32)[:, None]
    starts = jnp.sum(jnp.where(before, used[None, :], 0), axis=1)
    place = rank + PACK * jnp.sum(
        jnp.where(own_prompt[:, None] == prompt_ids[None, :], starts[None, :prompts], 0), axis=1
    )
    chosen = jnp.arange(places, dtype=jnp.int32)[:, None] == place[None, :]
    perm = chosen.astype(jnp.bfloat16)
    lens = jnp.sum(jnp.where(chosen, own_len[None, :], 0), axis=1)
    longest = jnp.max(lens.reshape(tile_count, PACK), axis=1)
    starts = jnp.where(is_decode, starts, 0)
    meta = jnp.concatenate(
        [starts, is_decode.astype(jnp.int32)[None], longest, seq_id[None]]
    ).astype(jnp.int32)
    q_sorted = jnp.einsum(
        "sr,jrc->jsc",
        perm,
        queries.reshape(STEPS, count, -1),
        preferred_element_type=jnp.float32,
    ).astype(jnp.bfloat16)
    own_sorted = jnp.einsum(
        "sr,jrc->jsc",
        perm,
        kv_flat.reshape(STEPS, count, -1),
        preferred_element_type=jnp.float32,
    ).astype(jnp.bfloat16)

    slot_table = page_table(prompt_lengths, page_owner, seq_size, tiles, capacity)
    mine = lax.dynamic_index_in_dim(slot_table, seq_id, 2, False)
    mine = jnp.where(is_decode, mine, -1).reshape(prompts, -1)

    done = prefill(my_lists, info, queries, wholes[0], kv_heads, share, score_scale)
    out = pages = None
    for hop in range(1, prompts + 1):
        final = hop == prompts
        if not final:
            meta, hops[hop + 1] = lax.optimization_barrier((meta, hops[hop + 1]))
        out, pages = decode(
            meta,
            mine,
            q_sorted,
            own_sorted,
            lens[:, None],
            wholes[hop - 1],
            out,
            pages,
            perm.T if final else None,
            done if final else None,
            prompts - hop,
            prompts,
            kv_heads,
            share,
            score_scale,
        )
    if tp_size == 2 * KVH:
        pages = lax.dynamic_slice_in_dim(pages, tp_id % 2 * HD, HD, 1)
    return (out, pages)


def solution(mesh):
    placed = (P(("group", "seq"), "tp"), P(("group", "seq"), "tp"), P(), P(), P(), P(), P())
    return jax.shard_map(
        body,
        mesh=mesh,
        in_specs=placed,
        out_specs=(P(("group", "seq"), "tp"), P(("group", "seq"), "tp")),
        check_vma=False,
    )
```
